32 devices in a mesh: circ: 2 (over x), len: 4 (over y, core), bank: 4 (over z).
Axes of the slice: x: 2, y: 2, z: 4, core: 2. Of those that a mesh axis runs over, the one named last changes fastest.
Arguments:
- feature_two: bfloat16 [16, 3072, 512], P('circ', ('len', 'bank')), may hold values from -18 to 18
- inner_three: bfloat16 [8, 1536, 512], P('circ', ('len', 'bank')), may hold values from -6 to 6
- skip_three: bfloat16 [8, 1536, 1024], P('circ', ('len', 'bank')), may hold values from -12 to 12
- out_weight: bfloat16 [512, 1024], replicated, may hold values from -0.25 to 0.25
- out_bias: float32 [1024], replicated, may hold values from -3 to 3
- bank_rows: bfloat16 [1280, 1536], P('bank'), may hold values from -6 to 6
- coreset_index: int32 [1024], P('bank'), may hold values from 0 to 319, as said below
Outputs:
- anomaly_map: float32 [16, 3072], P('circ', ('len', 'bank'))
The draws below stay inside these ranges and needn't reach their ends.
Inputs may be any that keep to these rules, and one draw needn't show every extreme that they name: `coreset_index`: each block of 256 entries names distinct rows among its shard's 320 bank rows.
All inputs are finite; a program needn't handle non-finite values.
Results may differ from the reference program's by a relative error of at most 0.0004.
Values may be sent and summed in bfloat16 or wider, within the bound.
A program may use at most 128 MiB of HBM per device.

```python
import math
import jax
import jax.numpy as jnp
from jax import lax

C2 = 512
C3 = 1024
CIN3 = 512
FEAT = 1536
NH2 = 16
NW2 = 3072
NH3 = 8
NW3 = 1536
CORE_DEV = 256
BANK_DEV = 320
CORES = 1024
BANK_ALL = 1280


def draw_coreset_index(key, part):
    shards = CORES // CORE_DEV

    def one_shard(shard_key):
        inside = jax.random.permutation(shard_key, BANK_DEV - 2)[:CORE_DEV - 2].astype(jnp.int32) + 1
        chosen = jnp.concatenate([jnp.array([0, BANK_DEV - 1], jnp.int32), inside])
        return jax.random.permutation(jax.random.fold_in(shard_key, 7), chosen).astype(jnp.int32)
    shard_keys = jax.random.split(jax.random.fold_in(key, 11), shards)
    return jax.vmap(one_shard)(shard_keys).reshape(CORES).astype(jnp.int32)


def draw_bank_rows(key, part):
    table_shape = (BANK_ALL, FEAT)
    row_key = jax.random.fold_in(key, 23)
    values = jnp.clip(jax.random.normal(row_key, table_shape, jnp.float32), -6.0, 6.0)
    return values.astype(jnp.bfloat16)


def block_levels(own_key, shape, cuts, smallest, top_value):
    factor_of, own = 1.0, jax.random.fold_in(own_key, 6)
    for dim, blocks in cuts:
        heights = jnp.exp(jax.random.uniform(jax.random.fold_in(own, dim), (blocks,), jnp.float32, smallest / len(cuts), top_value / len(cuts)))
        factor_of = factor_of * jnp.repeat(heights, shape[dim] // blocks).reshape([-1 if axis == dim else 1 for axis in range(len(shape))])
    return factor_of


def bell_draw(stream_key, shape, scale, reach, cuts=(), held_as=jnp.bfloat16):
    level = block_levels(stream_key, shape, cuts, -0.22, 0.18) if cuts else 1.0
    drawn = jax.random.normal(stream_key, shape, jnp.float32) * scale * level
    return jnp.minimum(jnp.maximum(drawn, -reach), reach).astype(held_as)


def setup_inputs(seed: int = 0) -> dict:
    keys = jax.random.split(jax.random.key(seed), 8)
    feature_two = bell_draw(keys[0], (NH2, NW2, C2), 3.0, 18.0, ((0, 2), (1, 16)))
    inner_three = bell_draw(keys[1], (NH3, NW3, CIN3), 1.0, 6.0, ((0, 2), (1, 16)))
    skip_three = bell_draw(keys[2], (NH3, NW3, C3), 2.0, 12.0, ((0, 2), (1, 16)))
    out_weight = bell_draw(keys[3], (CIN3, C3), CIN3 ** -0.5, 0.25)
    out_bias = bell_draw(keys[4], (C3,), 0.5, 3.0, (), jnp.float32)
    bank_rows = draw_bank_rows(jax.random.fold_in(keys[7], 71), 0)
    coreset_index = draw_coreset_index(jax.random.fold_in(keys[7], 71), 0)
    return {"feature_two": feature_two, "inner_three": inner_three, "skip_three": skip_three, "out_weight": out_weight, "out_bias": out_bias, "bank_rows": bank_rows, "coreset_index": coreset_index}


RAW_TAPS = [math.exp(-0.5 * (t - 2) * (t - 2)) for t in range(5)]
BLUR_TAPS = [value / sum(RAW_TAPS) for value in RAW_TAPS]


def box_mean(extended, height_out, width_out):
    summed = None
    for row_shift in range(3):
        for col_shift in range(3):
            shifted = extended[row_shift:row_shift + height_out, col_shift:col_shift + width_out].astype(jnp.float32)
            summed = shifted if summed is None else summed + shifted
    return summed / 9.0


def upsample(padded):
    middle = padded[1:-1]
    upper_rows = 0.75 * middle + 0.25 * padded[:-2]
    lower_rows = 0.75 * middle + 0.25 * padded[2:]
    stretched = jnp.stack([upper_rows, lower_rows], axis=1).reshape(-1, padded.shape[1], padded.shape[2])
    center = stretched[:, 1:-1]
    leftside = 0.75 * center + 0.25 * stretched[:, :-2]
    rightside = 0.75 * center + 0.25 * stretched[:, 2:]
    return jnp.stack([leftside, rightside], axis=2).reshape(stretched.shape[0], -1, padded.shape[2])


def nearest(patches, patch_norms, centers, running):
    center_wide = centers.astype(jnp.float32)
    center_norms = jnp.sum(center_wide * center_wide, axis=1)
    products = jnp.dot(patches, centers.T, preferred_element_type=jnp.float32)
    distance = patch_norms[:, None] - 2.0 * products + center_norms[None, :]
    return jnp.minimum(running, jnp.min(distance, axis=1))


def smooth_map(extended, height_out, width_out):
    stretched = None
    for shift in range(5):
        term = BLUR_TAPS[shift] * extended[shift:shift + height_out]
        stretched = term if stretched is None else stretched + term
    result = None
    for shift in range(5):
        term = BLUR_TAPS[shift] * stretched[:, shift:shift + width_out]
        result = term if result is None else result + term
    return result


def reference(feature_two, inner_three, skip_three, out_weight, out_bias, bank_rows, coreset_index):
    linear = jnp.dot(inner_three.reshape(NH3 * NW3, CIN3), out_weight, preferred_element_type=jnp.float32).reshape(NH3, NW3, C3)
    layer_three = jax.nn.relu(linear + out_bias + skip_three.astype(jnp.float32)).astype(jnp.bfloat16)
    padded_three = jnp.pad(jnp.pad(layer_three, ((1, 1), (0, 0), (0, 0)), mode="wrap"), ((0, 0), (1, 1), (0, 0)))

    def pool_row(row_index):
        band = lax.dynamic_slice_in_dim(padded_three, row_index, 3, 0)
        return box_mean(band, 1, NW3)[0].astype(jnp.bfloat16)

    pooled_three = lax.map(pool_row, jnp.arange(NH3, dtype=jnp.int32))
    padded_pool = jnp.pad(jnp.pad(pooled_three, ((1, 1), (0, 0), (0, 0)), mode="wrap"), ((0, 0), (1, 1), (0, 0)), mode="edge")
    padded_two = jnp.pad(jnp.pad(feature_two, ((1, 1), (0, 0), (0, 0)), mode="wrap"), ((0, 0), (1, 1), (0, 0)))
    offsets = (jnp.arange(CORES, dtype=jnp.int32) // CORE_DEV) * BANK_DEV
    coreset = jnp.take(bank_rows, offsets + coreset_index.astype(jnp.int32), axis=0)

    def score_rows(row_index):
        band_two = lax.dynamic_slice_in_dim(padded_two, 2 * row_index, 4, 0)
        pooled_two = box_mean(band_two, 2, NW2)
        band_three = lax.dynamic_slice_in_dim(padded_pool, row_index, 3, 0).astype(jnp.float32)
        upsampled = upsample(band_three)
        patches = jnp.concatenate([pooled_two, upsampled], axis=-1).astype(jnp.bfloat16).reshape(2 * NW2, FEAT)
        widened = patches.astype(jnp.float32)
        patch_norms = jnp.sum(widened * widened, axis=1)
        start_min = jnp.full((2 * NW2,), jnp.inf, jnp.float32)
        closest = nearest(patches, patch_norms, coreset, start_min)
        return (closest / FEAT).reshape(2, NW2)

    scores = lax.map(score_rows, jnp.arange(NH3, dtype=jnp.int32)).reshape(NH2, NW2)
    extended = jnp.pad(jnp.pad(scores, ((2, 2), (0, 0)), mode="wrap"), ((0, 0), (2, 2)))
    return smooth_map(extended, NH2, NW2)
```

```python
import math

import jax
import jax.numpy as jnp
from jax import lax
from jax.experimental import pallas as pl
from jax.experimental.pallas import tpu as pltpu
from jax.sharding import PartitionSpec as P

RAW_TAPS = [math.exp(-0.5 * (t - 2) * (t - 2)) for t in range(5)]
BLUR_TAPS = [value / sum(RAW_TAPS) for value in RAW_TAPS]
MESH = pl.DeviceIdType.MESH
F32 = jnp.float32
BF16 = jnp.bfloat16
VMEM = pltpu.VMEM


def places():
    circ, span, bank = (lax.axis_index(a) for a in ("circ", "len", "bank"))
    n_circ, n_len, n_bank = (lax.axis_size(a) for a in ("circ", "len", "bank"))
    up, down = lax.rem(circ + n_circ - 1, n_circ), lax.rem(circ + 1, n_circ)
    total = n_len * n_bank
    flat = span * n_bank + bank
    before, after = lax.rem(flat + total - 1, total), lax.rem(flat + 1, total)
    left = (before // n_bank, lax.rem(before, n_bank))
    right = (after // n_bank, lax.rem(after, n_bank))
    sides = [(circ,) + left, (circ,) + right]
    corners = [(c,) + s for s in (left, right) for c in (up, down)]
    return (up, span, bank), (down, span, bank), sides, corners, flat == 0, flat == total - 1


def meet(devices):
    barrier = pltpu.get_barrier_semaphore()
    for device in devices:
        pl.semaphore_signal(barrier, inc=1, device_id=device, device_id_type=MESH)
    pl.semaphore_wait(barrier, len(devices))


def travel(own, feature, layer, pack, others, f_up, f_down, l_up, l_down, packs,
           z_send, z_recv, y_send, y_recv, c_send, c_recv, h_send, h_recv):
    circ, span, bank = (lax.axis_index(a) for a in ("circ", "len", "bank"))
    n_len, n_bank = lax.axis_size("len"), lax.axis_size("bank")
    up, down, sides, corners, _, _ = places()
    across = lax.rem(span + 2, n_len)
    mate = (span // 2) * 2 + 1 - lax.rem(span, 2)
    mate_across = lax.rem(mate + 2, n_len)
    z_peers = [(circ, span, lax.rem(bank + d, n_bank)) for d in range(1, n_bank)]
    y_peer, c_peer = (circ, across, bank), (circ, mate, bank)
    meet([up, down] + sides + corners + z_peers + [y_peer, c_peer])
    piece = own.shape[0] // n_len

    def rows(owner):
        return pl.ds(pl.multiple_of(owner * piece, piece), piece)

    def send(src, dst, s, r, device):
        return pltpu.make_async_remote_copy(src, dst, s, r, device_id=device, device_id_type=MESH)

    z = [send(own.at[rows(span)], others.at[d, rows(span)], z_send.at[d], z_recv.at[d], z_peers[d])
         for d in range(n_bank - 1)]
    height = feature.shape[0]
    deep = layer.shape[0]
    halo = [
        (layer.at[deep - 2:deep], l_up, down), (layer.at[0:2], l_down, up),
        (feature.at[height - 1:height], f_up, down), (feature.at[0:1], f_down, up),
        (pack, packs.at[3], sides[0]), (pack, packs.at[0], sides[1]),
        (pack, packs.at[5], corners[0]), (pack, packs.at[4], corners[1]),
        (pack, packs.at[2], corners[2]), (pack, packs.at[1], corners[3]),
    ]
    h = [send(s, d, h_send.at[i], h_recv.at[i], to) for i, (s, d, to) in enumerate(halo)]
    for copy in z:
        copy.start()
    for copy in h:
        copy.start()
    y, c = [], []
    for d in range(n_bank - 1):
        z[d].wait_recv()
        here = others.at[d, rows(span)]
        y.append(send(here, here, y_send.at[d], y_recv.at[d], y_peer))
        y[-1].start()
        c.append(send(here, here, c_send.at[d], c_recv.at[d], c_peer))
        c[-1].start()
    for d in range(n_bank - 1):
        y[d].wait_recv()
        here = others.at[d, rows(across)]
        k = n_bank - 1 + d
        c.append(send(here, here, c_send.at[k], c_recv.at[k], c_peer))
        c[-1].start()
    for copy in c:
        copy.wait_recv()
    for copy in h:
        copy.wait_recv()
    for copy in z + y + c + h:
        copy.wait_send()


def shift_rows(x, by, edge):
    n = x.shape[0]
    moved = pltpu.roll(x, by % n, 0)
    at = 0 if by == 1 else n - 1
    return jnp.where(lax.broadcasted_iota(jnp.int32, x.shape, 0) == at, edge, moved)


def score(feature, layer, f_up, f_down, l_up, l_down, packs, own, others, out, pooled):
    _, _, _, _, at_start, at_end = places()
    height, width, c2 = feature.shape
    deep, wide, c3 = layer.shape
    lead = jnp.where(at_start, 0.0, 1.0)
    trail = jnp.where(at_end, 0.0, 1.0)
    pk = [packs[i].astype(F32) * (lead if i < 3 else trail) for i in range(6)]

    def f_row(r):
        return (f_up[0] if r < 0 else f_down[0] if r >= height else feature[r]).astype(F32)

    def l_row(r):
        return (l_up[r + 2] if r < 0 else l_down[r - deep] if r >= deep else layer[r]).astype(F32)

    def pick(side, r, depth):
        which = side * 3 + (1 if r < 0 else 2 if r >= depth else 0)
        return pk[which], r % depth

    def f_edge(side, r):
        package, row = pick(side, r, height)
        at = row + (8 if side == 0 else 0)
        return package[at:at + 1, :c2]

    def l_edge(side, r, column):
        package, row = pick(side, r, deep)
        at = 2 * row + column + (8 if side == 0 else 0)
        return package[at:at + 1, c2:]

    q_lead, q_trail = [], []
    for k in range(-1, deep + 1):
        s = l_row(k - 1) + l_row(k) + l_row(k + 1)
        e = [[sum(l_edge(side, k + t, column) for t in (-1, 0, 1)) for column in (0, 1)] for side in (0, 1)]
        q = ((s + shift_rows(s, 1, e[0][1]) + shift_rows(s, -1, e[1][0])) / 9.0).astype(BF16)
        pooled[k + 1] = q
        first = ((e[0][0] + e[0][1] + s[0:1]) / 9.0).astype(BF16).astype(F32)
        last = ((s[wide - 1:wide] + e[1][0] + e[1][1]) / 9.0).astype(BF16).astype(F32)
        qf = q.astype(F32)
        q_lead.append(jnp.where(at_start, qf[0:1], first))
        q_trail.append(jnp.where(at_end, qf[wide - 1:wide], last))

    i = lax.broadcasted_iota(jnp.int32, (width, wide), 0)
    j = lax.broadcasted_iota(jnp.int32, (width, wide), 1)
    k = i // 2
    near = k - 1 + 2 * (i % 2)
    stretch = jnp.where(j == k, 0.75, jnp.where(j == near, 0.25, 0.0)).astype(F32)
    main_w = (0.75 * stretch).astype(BF16)
    side_w = (0.25 * stretch).astype(BF16)
    row_id = lax.broadcasted_iota(jnp.int32, (width, c3), 0)
    norms = []
    for part in range(4):
        c = (own[...] if part == 0 else others[part - 1]).astype(F32)
        norms.append(jnp.sum(c * c, axis=1, keepdims=True))
    ones = jnp.ones((8, 128), F32)
    for r in range(height):
        s = f_row(r - 1) + f_row(r) + f_row(r + 1)
        e = [sum(f_edge(side, r + t) for t in (-1, 0, 1)) for side in (0, 1)]
        two = ((s + shift_rows(s, 1, e[0]) + shift_rows(s, -1, e[1])) / 9.0).astype(BF16)
        a = r // 2 + 1
        b = a + (1 if r % 2 else -1)
        u = jnp.dot(main_w, pooled[a], preferred_element_type=F32)
        u = u + jnp.dot(side_w, pooled[b], preferred_element_type=F32)
        begin = 0.25 * (0.75 * q_lead[a] + 0.25 * q_lead[b])
        end = 0.25 * (0.75 * q_trail[a] + 0.25 * q_trail[b])
        u = u + jnp.where(row_id == 0, begin, 0.0) + jnp.where(row_id == width - 1, end, 0.0)
        patch = jnp.concatenate([two, u.astype(BF16)], axis=1)
        wide_patch = patch.astype(F32)
        square = wide_patch * wide_patch
        folded = sum(square[:, t:t + 128] for t in range(0, c2 + c3, 128))
        size = lax.dot_general(ones, folded, (((1,), (1,)), ((), ())),
                               precision=lax.Precision.HIGHEST, preferred_element_type=F32)[0:1]
        best = None
        for part in range(4):
            c = own[...] if part == 0 else others[part - 1]
            product = lax.dot_general(c, patch, (((1,), (1,)), ((), ())), preferred_element_type=F32)
            low = jnp.min(norms[part] - 2.0 * product, axis=0, keepdims=True)
            best = low if best is None else jnp.minimum(best, low)
        out[r:r + 1, :] = (size + best) / (c2 + c3)


def smooth(scores, out, tiles, h_send, h_recv):
    up, down, sides, corners, at_start, at_end = places()
    meet([up, down] + sides + corners)
    plan = [(0, down), (1, up), (5, sides[0]), (2, sides[1]), (7, corners[0]), (6, corners[1]),
            (4, corners[2]), (3, corners[3])]
    copies = [
        pltpu.make_async_remote_copy(scores, tiles.at[slot], h_send.at[slot], h_recv.at[slot],
                                     device_id=to, device_id_type=MESH)
        for slot, to in plan
    ]
    for copy in copies:
        copy.start()
    for copy in copies:
        copy.wait_recv()
    height, width = scores.shape

    def taps(gap):
        found = jnp.zeros(gap.shape, F32)
        for t in range(5):
            found = jnp.where(gap == t - 2, BLUR_TAPS[t], found)
        return found

    def band(shape, offset):
        i = lax.broadcasted_iota(jnp.int32, shape, 0)
        j = lax.broadcasted_iota(jnp.int32, shape, 1)
        return taps(j - i + offset)

    def dot(a, b):
        return jnp.dot(a, b, precision=lax.Precision.HIGHEST, preferred_element_type=F32)

    vertical = band((height, 3 * height), -height)
    middle = dot(vertical, jnp.concatenate([tiles[0], scores[...], tiles[1]], axis=0))
    left = dot(vertical, jnp.concatenate([tiles[3], tiles[2], tiles[4]], axis=0))
    right = dot(vertical, jnp.concatenate([tiles[6], tiles[5], tiles[7]], axis=0))
    left = left * jnp.where(at_start, 0.0, 1.0)
    right = right * jnp.where(at_end, 0.0, 1.0)
    square = (width, width)
    out[...] = dot(middle, band(square, 0)) + dot(left, band(square, width)) + dot(right, band(square, -width))
    for copy in copies:
        copy.wait_send()


def shards(feature_two, inner_three, skip_three, out_weight, out_bias, bank_rows, coreset_index):
    height, width, c2 = feature_two.shape
    deep, wide, c3 = skip_three.shape
    n_bank = lax.axis_size("bank")
    pick = (coreset_index[:, None] == jnp.arange(bank_rows.shape[0], dtype=jnp.int32)[None, :]).astype(BF16)
    own = jnp.dot(pick, bank_rows, preferred_element_type=F32).astype(BF16)
    linear = jnp.dot(inner_three.reshape(deep * wide, -1), out_weight, preferred_element_type=F32)
    layer = jax.nn.relu(linear.reshape(deep, wide, -1) + out_bias + skip_three.astype(F32)).astype(BF16)
    pack = jnp.concatenate(
        [
            jnp.concatenate([feature_two[:, 0], feature_two[:, width - 1]], axis=0),
            jnp.concatenate(
                [layer[:, :2].reshape(2 * deep, c3), layer[:, wide - 2:].reshape(2 * deep, c3)], axis=0
            ),
        ],
        axis=1,
    )
    vm = pl.BlockSpec(memory_space=VMEM)
    dma = pltpu.SemaphoreType.DMA
    cores = own.shape[0]
    shape = jax.ShapeDtypeStruct
    others, f_up, f_down, l_up, l_down, packs = pl.pallas_call(
        travel,
        out_shape=[
            shape((n_bank - 1, cores, c2 + c3), BF16),
            shape((1, width, c2), BF16), shape((1, width, c2), BF16),
            shape((2, wide, c3), BF16), shape((2, wide, c3), BF16),
            shape((6,) + pack.shape, BF16),
        ],
        in_specs=[vm] * 4,
        out_specs=[vm] * 6,
        scratch_shapes=[dma((n_bank - 1,))] * 4 + [dma((2 * (n_bank - 1),))] * 2 + [dma((10,))] * 2,
        compiler_params=pltpu.CompilerParams(
            collective_id=0, has_side_effects=True, vmem_limit_bytes=40 * 2**20),
    )(own, feature_two, layer, pack)
    scores = pl.pallas_call(
        score,
        out_shape=shape((height, width), F32),
        in_specs=[vm] * 9,
        out_specs=vm,
        scratch_shapes=[VMEM((deep + 2, wide, c3), BF16)],
        compiler_params=pltpu.CompilerParams(vmem_limit_bytes=48 * 2**20),
    )(feature_two, layer, f_up, f_down, l_up, l_down, packs, own, others)
    return pl.pallas_call(
        smooth,
        out_shape=shape((height, width), F32),
        in_specs=[vm],
        out_specs=vm,
        scratch_shapes=[VMEM((8, height, width), F32), dma((8,)), dma((8,))],
        compiler_params=pltpu.CompilerParams(collective_id=1, has_side_effects=True),
    )(scores)


def solution(mesh):
    in_specs = (
        P("circ", ("len", "bank"), None),
        P("circ", ("len", "bank"), None),
        P("circ", ("len", "bank"), None),
        P(),
        P(),
        P("bank", None),
        P("bank"),
    )
    out_specs = P("circ", ("len", "bank"))
    return jax.shard_map(shards, mesh=mesh, in_specs=in_specs, out_specs=out_specs, check_vma=False)
```

```python
import math

import jax
import jax.numpy as jnp
from jax import lax
from jax.experimental import pallas as pl
from jax.experimental.pallas import tpu as pltpu
from jax.sharding import PartitionSpec as P

RAW_TAPS = [math.exp(-0.5 * (t - 2) * (t - 2)) for t in range(5)]
BLUR_TAPS = [value / sum(RAW_TAPS) for value in RAW_TAPS]
MESH = pl.DeviceIdType.MESH
F32 = jnp.float32
BF16 = jnp.bfloat16
VMEM = pltpu.VMEM


def places():
    circ, span, bank = (lax.axis_index(a) for a in ("circ", "len", "bank"))
    n_circ, n_len, n_bank = (lax.axis_size(a) for a in ("circ", "len", "bank"))
    up, down = lax.rem(circ + n_circ - 1, n_circ), lax.rem(circ + 1, n_circ)
    total = n_len * n_bank
    flat = span * n_bank + bank
    before, after = lax.rem(flat + total - 1, total), lax.rem(flat + 1, total)
    left = (before // n_bank, lax.rem(before, n_bank))
    right = (after // n_bank, lax.rem(after, n_bank))
    sides = [(circ,) + left, (circ,) + right]
    corners = [(c,) + s for s in (left, right) for c in (up, down)]
    return (up, span, bank), (down, span, bank), sides, corners, flat == 0, flat == total - 1


def meet(devices):
    barrier = pltpu.get_barrier_semaphore()
    for device in devices:
        pl.semaphore_signal(barrier, inc=1, device_id=device, device_id_type=MESH)
    pl.semaphore_wait(barrier, len(devices))


def shift_rows(x, by, edge):
    n = x.shape[0]
    moved = pltpu.roll(x, by % n, 0)
    at = 0 if by == 1 else n - 1
    return jnp.where(lax.broadcasted_iota(jnp.int32, x.shape, 0) == at, edge, moved)


def send(src, dst, s, r, device):
    return pltpu.make_async_remote_copy(src, dst, s, r, device_id=device, device_id_type=MESH)


def roll_map(feature, inner, skip, weight, bias, bank_rows, index, out,
             layer, pack, cores, f_halo, l_halo, packs, pooled, patches, sizes, bests, scores, tiles,
             z_send, z_recv, y_send, y_recv, c_send, c_recv, h_send, h_recv, t_send, t_recv):
    circ, span, bank = (lax.axis_index(a) for a in ("circ", "len", "bank"))
    n_len, n_bank = lax.axis_size("len"), lax.axis_size("bank")
    up, down, sides, corners, at_start, at_end = places()
    across = lax.rem(span + 2, n_len)
    mate = (span // 2) * 2 + 1 - lax.rem(span, 2)
    z_peers = [(circ, span, lax.rem(bank + d, n_bank)) for d in range(1, n_bank)]
    y_peer, c_peer = (circ, across, bank), (circ, mate, bank)
    meet([up, down] + sides + corners + z_peers + [y_peer, c_peer])
    height, width, c2 = feature.shape
    deep, wide, c3 = skip.shape
    piece = cores.shape[1] // n_len

    def rows(owner):
        return pl.ds(pl.multiple_of(owner * piece, piece), piece)

    halo = [
        (layer.at[deep - 1], l_halo.at[1], down), (layer.at[0], l_halo.at[2], up),
        (feature.at[height - 1], f_halo.at[0], down), (feature.at[0], f_halo.at[1], up),
        (layer.at[deep - 2], l_halo.at[0], down), (layer.at[1], l_halo.at[3], up),
        (pack, packs.at[3], sides[0]), (pack, packs.at[0], sides[1]),
        (pack, packs.at[5], corners[0]), (pack, packs.at[4], corners[1]),
        (pack, packs.at[2], corners[2]), (pack, packs.at[1], corners[3]),
    ]
    h = [send(s, d, h_send.at[i], h_recv.at[i], to) for i, (s, d, to) in enumerate(halo)]

    sixteen = lax.broadcasted_iota(jnp.int32, (16, c3), 0)
    packed = jnp.zeros((16, c3), F32)
    for r in [deep - 1, 0] + list(range(1, deep - 1)):
        linear = jnp.dot(inner[r], weight[...], preferred_element_type=F32)
        value = jnp.maximum(linear + bias[...] + skip[r].astype(F32), 0.0).astype(BF16)
        layer[r] = value
        value = value.astype(F32)
        for column in (0, 1):
            packed = jnp.where(sixteen == 2 * r + column, value[column:column + 1], packed)
            at = wide - 2 + column
            packed = jnp.where(sixteen == 8 + 2 * r + column, value[at:at + 1], packed)
        if r == deep - 1:
            h[0].start()
        if r == 0:
            h[1].start()
            h[2].start()
            h[3].start()
    pack[:, c2:] = packed.astype(BF16)
    sixteen = lax.broadcasted_iota(jnp.int32, (16, c2), 0)
    packed = jnp.zeros((16, c2), F32)
    for r in range(height):
        packed = jnp.where(sixteen == r, feature[r, 0:16].astype(F32)[0:1], packed)
        packed = jnp.where(sixteen == 8 + r, feature[r, width - 16:width].astype(F32)[15:16], packed)
    pack[:, :c2] = packed.astype(BF16)
    for copy in h[6:]:
        copy.start()

    chosen = index[...] == lax.broadcasted_iota(jnp.int32, (cores.shape[1], bank_rows.shape[0]), 1)
    cores[0] = jnp.dot(jnp.where(chosen, 1.0, 0.0).astype(BF16), bank_rows[...],
                       preferred_element_type=F32).astype(BF16)
    z = [send(cores.at[0, rows(span)], cores.at[d + 1, rows(span)], z_send.at[d], z_recv.at[d], z_peers[d])
         for d in range(n_bank - 1)]
    for copy in z:
        copy.start()

    lead = jnp.where(at_start, 0.0, 1.0)
    trail = jnp.where(at_end, 0.0, 1.0)
    for copy in h[6:]:
        copy.wait_recv()
    pk = [packs[i].astype(F32) * (lead if i < 3 else trail) for i in range(6)]

    def f_row(r):
        return (f_halo[0] if r < 0 else f_halo[1] if r >= height else feature[r]).astype(F32)

    def l_row(r):
        return (l_halo[r + 2] if r < 0 else l_halo[2 + r - deep] if r >= deep else layer[r]).astype(F32)

    def pick(side, r, depth):
        which = side * 3 + (1 if r < 0 else 2 if r >= depth else 0)
        return pk[which], r % depth

    def f_edge(side, r):
        package, row = pick(side, r, height)
        at = row + (8 if side == 0 else 0)
        return package[at:at + 1, :c2]

    def l_edge(side, r, column):
        package, row = pick(side, r, deep)
        at = 2 * row + column + (8 if side == 0 else 0)
        return package[at:at + 1, c2:]

    q_lead, q_trail = {}, {}

    def pool_three(k):
        s = l_row(k - 1) + l_row(k) + l_row(k + 1)
        e = [[sum(l_edge(side, k + t, column) for t in (-1, 0, 1)) for column in (0, 1)] for side in (0, 1)]
        q = ((s + shift_rows(s, 1, e[0][1]) + shift_rows(s, -1, e[1][0])) / 9.0).astype(BF16)
        pooled[k + 1] = q
        first = ((e[0][0] + e[0][1] + s[0:1]) / 9.0).astype(BF16).astype(F32)
        last = ((s[wide - 1:wide] + e[1][0] + e[1][1]) / 9.0).astype(BF16).astype(F32)
        qf = q.astype(F32)
        q_lead[k + 1] = jnp.where(at_start, qf[0:1], first)
        q_trail[k + 1] = jnp.where(at_end, qf[wide - 1:wide], last)

    i = lax.broadcasted_iota(jnp.int32, (width, wide), 0)
    j = lax.broadcasted_iota(jnp.int32, (width, wide), 1)
    k = i // 2
    near = k - 1 + 2 * (i % 2)
    stretch = jnp.where(j == k, 0.75, jnp.where(j == near, 0.25, 0.0)).astype(F32)
    main_w = (0.75 * stretch).astype(BF16)
    side_w = (0.25 * stretch).astype(BF16)
    row_id = lax.broadcasted_iota(jnp.int32, (width, c3), 0)
    ones = jnp.ones((8, 128), F32)

    def make_patch(r):
        s = f_row(r - 1) + f_row(r) + f_row(r + 1)
        e = [sum(f_edge(side, r + t) for t in (-1, 0, 1)) for side in (0, 1)]
        two = ((s + shift_rows(s, 1, e[0]) + shift_rows(s, -1, e[1])) / 9.0).astype(BF16)
        a = r // 2 + 1
        b = a + (1 if r % 2 else -1)
        u = jnp.dot(main_w, pooled[a], preferred_element_type=F32)
        u = u + jnp.dot(side_w, pooled[b], preferred_element_type=F32)
        begin = 0.25 * (0.75 * q_lead[a] + 0.25 * q_lead[b])
        end = 0.25 * (0.75 * q_trail[a] + 0.25 * q_trail[b])
        u = u + jnp.where(row_id == 0, begin, 0.0) + jnp.where(row_id == width - 1, end, 0.0)
        patch = jnp.concatenate([two, u.astype(BF16)], axis=1)
        patches[r] = patch
        wide_patch = patch.astype(F32)
        square = wide_patch * wide_patch
        folded = sum(square[:, t:t + 128] for t in range(0, c2 + c3, 128))
        sizes[r] = lax.dot_general(ones, folded, (((1,), (1,)), ((), ())),
                                   precision=lax.Precision.HIGHEST, preferred_element_type=F32)

    for k in range(1, deep - 1):
        pool_three(k)
    for r in range(3, height - 3):
        make_patch(r)
    y, c = [], []
    for d in range(n_bank - 1):
        z[d].wait_recv()
        here = cores.at[d + 1, rows(span)]
        y.append(send(here, here, y_send.at[d], y_recv.at[d], y_peer))
        y[-1].start()
        c.append(send(here, here, c_send.at[d], c_recv.at[d], c_peer))
        c[-1].start()
    h[4].start()
    h[5].start()
    h[0].wait_recv()
    h[1].wait_recv()
    pool_three(0)
    pool_three(deep - 1)
    for r in [1, 2, height - 3, height - 2]:
        make_patch(r)
    for d in range(n_bank - 1):
        y[d].wait_recv()
        here = cores.at[d + 1, rows(across)]
        e = n_bank - 1 + d
        c.append(send(here, here, c_send.at[e], c_recv.at[e], c_peer))
        c[-1].start()
    for copy in c:
        copy.wait_recv()

    norms = []
    for part in range(n_bank):
        wide_core = cores[part].astype(F32)
        norms.append(jnp.sum(wide_core * wide_core, axis=1, keepdims=True))

    def score_row(r, carry):
        patch = patches[r]
        best = None
        for part in range(n_bank):
            product = lax.dot_general(cores[part], patch, (((1,), (1,)), ((), ())), preferred_element_type=F32)
            low = jnp.min(norms[part] - 2.0 * product, axis=0, keepdims=True)
            best = low if best is None else jnp.minimum(best, low)
        bests[r] = jnp.broadcast_to(best, bests.shape[1:])
        return carry

    lax.fori_loop(1, height - 1, score_row, 0)
    for copy in h[2:6]:
        copy.wait_recv()
    pool_three(-1)
    pool_three(deep)
    make_patch(0)
    make_patch(height - 1)
    lax.fori_loop(0, 2, lambda n, carry: score_row(n * (height - 1), carry), 0)

    eight = lax.broadcasted_iota(jnp.int32, (height, width), 0)
    found = jnp.zeros((height, width), F32)
    for r in range(height):
        found = jnp.where(eight == r, (sizes[r][0:1] + bests[r][0:1]) / (c2 + c3), found)
    scores[...] = found
    plan = [(0, down), (1, up), (5, sides[0]), (2, sides[1]), (7, corners[0]), (6, corners[1]),
            (4, corners[2]), (3, corners[3])]
    t = [send(scores, tiles.at[slot], t_send.at[slot], t_recv.at[slot], to) for slot, to in plan]
    for copy in t:
        copy.start()

    def taps(gap):
        weights = jnp.zeros(gap.shape, F32)
        for n in range(5):
            weights = jnp.where(gap == n - 2, BLUR_TAPS[n], weights)
        return weights

    def band(shape, offset):
        i = lax.broadcasted_iota(jnp.int32, shape, 0)
        j = lax.broadcasted_iota(jnp.int32, shape, 1)
        return taps(j - i + offset)

    def dot(a, b):
        return jnp.dot(a, b, precision=lax.Precision.HIGHEST, preferred_element_type=F32)

    vertical = band((height, 3 * height), -height)
    bands = [band((width, width), offset) for offset in (0, width, -width)]
    for copy in z + y + c + h:
        copy.wait_send()
    for copy in t:
        copy.wait_recv()
    middle = dot(vertical, jnp.concatenate([tiles[0], found, tiles[1]], axis=0))
    left = dot(vertical, jnp.concatenate([tiles[3], tiles[2], tiles[4]], axis=0)) * lead
    right = dot(vertical, jnp.concatenate([tiles[6], tiles[5], tiles[7]], axis=0)) * trail
    out[...] = dot(middle, bands[0]) + dot(left, bands[1]) + dot(right, bands[2])
    for copy in t:
        copy.wait_send()


def shards(feature_two, inner_three, skip_three, out_weight, out_bias, bank_rows, coreset_index):
    height, width, c2 = feature_two.shape
    deep, wide, c3 = skip_three.shape
    n_bank = lax.axis_size("bank")
    cores = coreset_index.shape[0]
    vm = pl.BlockSpec(memory_space=VMEM)
    dma = pltpu.SemaphoreType.DMA
    return pl.pallas_call(
        roll_map,
        out_shape=jax.ShapeDtypeStruct((height, width), F32),
        in_specs=[vm] * 7,
        out_specs=vm,
        scratch_shapes=[
            VMEM((deep, wide, c3), BF16),
            VMEM((16, c2 + c3), BF16),
            VMEM((n_bank, cores, c2 + c3), BF16),
            VMEM((2, width, c2), BF16),
            VMEM((4, wide, c3), BF16),
            VMEM((6, 16, c2 + c3), BF16),
            VMEM((deep + 2, wide, c3), BF16),
            VMEM((height, width, c2 + c3), BF16),
            VMEM((height, 8, width), F32),
            VMEM((height, 8, width), F32),
            VMEM((height, width), F32),
            VMEM((8, height, width), F32),
        ] + [dma((n_bank - 1,))] * 4 + [dma((2 * (n_bank - 1),))] * 2 + [dma((12,))] * 2 + [dma((8,))] * 2,
        compiler_params=pltpu.CompilerParams(
            collective_id=0, has_side_effects=True, vmem_limit_bytes=48 * 2**20),
    )(feature_two, inner_three, skip_three, out_weight, out_bias[None, :], bank_rows, coreset_index[:, None])


def solution(mesh):
    in_specs = (
        P("circ", ("len", "bank"), None),
        P("circ", ("len", "bank"), None),
        P("circ", ("len", "bank"), None),
        P(),
        P(),
        P("bank", None),
        P("bank"),
    )
    out_specs = P("circ", ("len", "bank"))
    return jax.shard_map(shards, mesh=mesh, in_specs=in_specs, out_specs=out_specs, check_vma=False)
```

```python
import math

import jax
import jax.numpy as jnp
from jax import lax
from jax.experimental import pallas as pl
from jax.experimental.pallas import tpu as pltpu
from jax.sharding import PartitionSpec as P

RAW_TAPS = [math.exp(-0.5 * (t - 2) * (t - 2)) for t in range(5)]
BLUR_TAPS = [value / sum(RAW_TAPS) for value in RAW_TAPS]
MESH = pl.DeviceIdType.MESH
F32 = jnp.float32
BF16 = jnp.bfloat16
VMEM = pltpu.VMEM


def places():
    circ, span, bank = (lax.axis_index(a) for a in ("circ", "len", "bank"))
    n_circ, n_len, n_bank = (lax.axis_size(a) for a in ("circ", "len", "bank"))
    up, down = lax.rem(circ + n_circ - 1, n_circ), lax.rem(circ + 1, n_circ)
    total = n_len * n_bank
    flat = span * n_bank + bank
    before, after = lax.rem(flat + total - 1, total), lax.rem(flat + 1, total)
    left = (before // n_bank, lax.rem(before, n_bank))
    right = (after // n_bank, lax.rem(after, n_bank))
    sides = [(circ,) + left, (circ,) + right]
    corners = [(c,) + s for s in (left, right) for c in (up, down)]
    return (up, span, bank), (down, span, bank), sides, corners, flat == 0, flat == total - 1


def meet(devices):
    barrier = pltpu.get_barrier_semaphore()
    for device in devices:
        pl.semaphore_signal(barrier, inc=1, device_id=device, device_id_type=MESH)
    pl.semaphore_wait(barrier, len(devices))


def shift_rows(x, by, edge):
    n = x.shape[0]
    moved = pltpu.roll(x, by % n, 0)
    at = 0 if by == 1 else n - 1
    return jnp.where(lax.broadcasted_iota(jnp.int32, x.shape, 0) == at, edge, moved)


def send(src, dst, s, r, device):
    return pltpu.make_async_remote_copy(src, dst, s, r, device_id=device, device_id_type=MESH)


def halves(x):
    high = x.astype(BF16)
    return [high, (x - high.astype(F32)).astype(BF16)]


def roll_map(feature_in, inner_in, skip_in, weight_in, bias, bank_in, index, out,
             feature, inner, skip, weight, bank_rows, load, layer, pack, cores, f_halo, l_halo, packs, pooled, patches, sizes, bests, scores, tiles,
             z_send, z_recv, y_send, y_recv, c_send, c_recv, h_send, h_recv, t_send, t_recv):
    circ, span, bank = (lax.axis_index(a) for a in ("circ", "len", "bank"))
    n_len, n_bank = lax.axis_size("len"), lax.axis_size("bank")
    up, down, sides, corners, at_start, at_end = places()
    across = lax.rem(span + 2, n_len)
    mate = (span // 2) * 2 + 1 - lax.rem(span, 2)
    z_peers = [(circ, span, lax.rem(bank + d, n_bank)) for d in range(1, n_bank)]
    y_peer, c_peer = (circ, across, bank), (circ, mate, bank)
    pairs = [(bank_in, bank_rows), (inner_in, inner), (weight_in, weight), (skip_in, skip), (feature_in, feature)]
    loads = [pltpu.make_async_copy(src, dst, load.at[n]) for n, (src, dst) in enumerate(pairs)]
    for copy in loads:
        copy.start()
    meet([up, down] + sides + corners + z_peers + [y_peer, c_peer])
    height, width, c2 = feature.shape
    deep, wide, c3 = skip.shape
    piece = cores.shape[1] // n_len

    def rows(owner):
        return pl.ds(pl.multiple_of(owner * piece, piece), piece)

    halo = [
        (layer.at[deep - 1], l_halo.at[1], down), (layer.at[0], l_halo.at[2], up),
        (feature_in.at[height - 1], f_halo.at[0], down), (feature_in.at[0], f_halo.at[1], up),
        (layer.at[deep - 2], l_halo.at[0], down), (layer.at[1], l_halo.at[3], up),
        (pack, packs.at[3], sides[0]), (pack, packs.at[0], sides[1]),
        (pack, packs.at[5], corners[0]), (pack, packs.at[4], corners[1]),
        (pack, packs.at[2], corners[2]), (pack, packs.at[1], corners[3]),
    ]
    h = [send(s, d, h_send.at[i], h_recv.at[i], to) for i, (s, d, to) in enumerate(halo)]

    h[2].start()
    h[3].start()
    chosen = index[...] == lax.broadcasted_iota(jnp.int32, (bank_rows.shape[0], cores.shape[1]), 0)
    loads[0].wait()
    cores[0] = lax.dot_general(jnp.where(chosen, 1.0, 0.0).astype(BF16), bank_rows[...],
                               (((0,), (0,)), ((), ())), preferred_element_type=F32).astype(BF16)
    z = [send(cores.at[0, rows(span)], cores.at[d + 1, rows(span)], z_send.at[d], z_recv.at[d], z_peers[d])
         for d in range(n_bank - 1)]
    for copy in z:
        copy.start()
    for copy in loads[1:]:
        copy.wait()

    sixteen = lax.broadcasted_iota(jnp.int32, (16, c3), 0)
    packed = jnp.zeros((16, c3), F32)
    for r in [deep - 1, 0] + list(range(1, deep - 1)):
        linear = jnp.dot(inner[r], weight[...], preferred_element_type=F32)
        value = jnp.maximum(linear + bias[...] + skip[r].astype(F32), 0.0).astype(BF16)
        layer[r] = value
        value = value.astype(F32)
        for column in (0, 1):
            packed = jnp.where(sixteen == 2 * r + column, value[column:column + 1], packed)
            at = wide - 2 + column
            packed = jnp.where(sixteen == 8 + 2 * r + column, value[at:at + 1], packed)
        if r == deep - 1:
            h[0].start()
        if r == 0:
            h[1].start()
    pack[:, c2:] = packed.astype(BF16)
    sixteen = lax.broadcasted_iota(jnp.int32, (16, c2), 0)
    packed = jnp.zeros((16, c2), F32)
    for r in range(height):
        packed = jnp.where(sixteen == r, feature[r, 0:16].astype(F32)[0:1], packed)
        packed = jnp.where(sixteen == 8 + r, feature[r, width - 16:width].astype(F32)[15:16], packed)
    pack[:, :c2] = packed.astype(BF16)
    for copy in h[6:]:
        copy.start()

    lead = jnp.where(at_start, 0.0, 1.0)
    trail = jnp.where(at_end, 0.0, 1.0)
    for copy in h[6:]:
        copy.wait_recv()
    pk = [packs[i].astype(F32) * (lead if i < 3 else trail) for i in range(6)]

    def f_row(r):
        return (f_halo[0] if r < 0 else f_halo[1] if r >= height else feature[r]).astype(F32)

    def l_row(r):
        return (l_halo[r + 2] if r < 0 else l_halo[2 + r - deep] if r >= deep else layer[r]).astype(F32)

    def pick(side, r, depth):
        which = side * 3 + (1 if r < 0 else 2 if r >= depth else 0)
        return pk[which], r % depth

    def f_edge(side, r):
        package, row = pick(side, r, height)
        at = row + (8 if side == 0 else 0)
        return package[at:at + 1, :c2]

    def l_edge(side, r, column):
        package, row = pick(side, r, deep)
        at = 2 * row + column + (8 if side == 0 else 0)
        return package[at:at + 1, c2:]

    q_lead, q_trail = {}, {}

    def pool_three(k):
        s = l_row(k - 1) + l_row(k) + l_row(k + 1)
        e = [[sum(l_edge(side, k + t, column) for t in (-1, 0, 1)) for column in (0, 1)] for side in (0, 1)]
        q = ((s + shift_rows(s, 1, e[0][1]) + shift_rows(s, -1, e[1][0])) * (1.0 / 9.0)).astype(BF16)
        pooled[k + 1] = q
        first = ((e[0][0] + e[0][1] + s[0:1]) * (1.0 / 9.0)).astype(BF16).astype(F32)
        last = ((s[wide - 1:wide] + e[1][0] + e[1][1]) * (1.0 / 9.0)).astype(BF16).astype(F32)
        qf = q.astype(F32)
        q_lead[k + 1] = jnp.where(at_start, qf[0:1], first)
        q_trail[k + 1] = jnp.where(at_end, qf[wide - 1:wide], last)

    i = lax.broadcasted_iota(jnp.int32, (width, wide), 0)
    j = lax.broadcasted_iota(jnp.int32, (width, wide), 1)
    k = i // 2
    near = k - 1 + 2 * (i % 2)
    stretch = jnp.where(j == k, 0.75, jnp.where(j == near, 0.25, 0.0)).astype(F32)
    main_w = (0.75 * stretch).astype(BF16)
    side_w = (0.25 * stretch).astype(BF16)
    row_id = lax.broadcasted_iota(jnp.int32, (8, c3), 0)
    ones = jnp.ones((8, 256), BF16)

    def make_patch(r):
        s = f_row(r - 1) + f_row(r) + f_row(r + 1)
        e = [sum(f_edge(side, r + t) for t in (-1, 0, 1)) for side in (0, 1)]
        two = ((s + shift_rows(s, 1, e[0]) + shift_rows(s, -1, e[1])) * (1.0 / 9.0)).astype(BF16)
        a = r // 2 + 1
        b = a + (1 if r % 2 else -1)
        u = jnp.dot(main_w, pooled[a], preferred_element_type=F32)
        u = u + jnp.dot(side_w, pooled[b], preferred_element_type=F32)
        begin = 0.25 * (0.75 * q_lead[a] + 0.25 * q_lead[b])
        end = 0.25 * (0.75 * q_trail[a] + 0.25 * q_trail[b])
        u = jnp.concatenate([u[:8] + jnp.where(row_id == 0, begin, 0.0), u[8:width - 8],
                             u[width - 8:] + jnp.where(row_id == 7, end, 0.0)], axis=0)
        patch = jnp.concatenate([two, u.astype(BF16)], axis=1)
        patches[r] = patch
        wide_patch = patch.astype(F32)
        square = wide_patch * wide_patch
        folded = sum(square[:, t:t + 128] for t in range(0, c2 + c3, 128))
        sizes[r] = lax.dot_general(ones, jnp.concatenate(halves(folded), axis=1), (((1,), (1,)), ((), ())),
                                   preferred_element_type=F32)

    for k in range(1, deep - 1):
        pool_three(k)
    for r in range(3, height - 3):
        make_patch(r)
    y, c = [], []
    for d in range(n_bank - 1):
        z[d].wait_recv()
        here = cores.at[d + 1, rows(span)]
        y.append(send(here, here, y_send.at[d], y_recv.at[d], y_peer))
        y[-1].start()
        c.append(send(here, here, c_send.at[d], c_recv.at[d], c_peer))
        c[-1].start()
    h[4].start()
    h[5].start()
    h[0].wait_recv()
    h[1].wait_recv()
    pool_three(0)
    pool_three(deep - 1)
    for r in [1, 2, height - 3, height - 2]:
        make_patch(r)
    for d in range(n_bank - 1):
        y[d].wait_recv()
        here = cores.at[d + 1, rows(across)]
        e = n_bank - 1 + d
        c.append(send(here, here, c_send.at[e], c_recv.at[e], c_peer))
        c[-1].start()
    for copy in c:
        copy.wait_recv()

    norms = []
    for part in range(n_bank):
        wide_core = cores[part].astype(F32)
        norms.append(jnp.sum(wide_core * wide_core, axis=1, keepdims=True))

    def score_row(r, carry):
        patch = patches[r]
        best = None
        for part in range(n_bank):
            product = lax.dot_general(cores[part], patch, (((1,), (1,)), ((), ())), preferred_element_type=F32)
            low = jnp.min(norms[part] - 2.0 * product, axis=0, keepdims=True)
            best = low if best is None else jnp.minimum(best, low)
        bests[r] = jnp.broadcast_to(best, bests.shape[1:])
        return carry

    lax.fori_loop(1, height - 1, score_row, 0)
    for copy in h[2:6]:
        copy.wait_recv()
    pool_three(-1)
    pool_three(deep)
    make_patch(0)
    make_patch(height - 1)
    lax.fori_loop(0, 2, lambda n, carry: score_row(n * (height - 1), carry), 0)

    eight = lax.broadcasted_iota(jnp.int32, (height, width), 0)
    found = jnp.zeros((height, width), F32)
    for r in range(height):
        found = jnp.where(eight == r, (sizes[r][0:1] + bests[r][0:1]) / (c2 + c3), found)
    scores[...] = found
    plan = [(0, down), (1, up), (5, sides[0]), (2, sides[1]), (7, corners[0]), (6, corners[1]),
            (4, corners[2]), (3, corners[3])]
    t = [send(scores, tiles.at[slot], t_send.at[slot], t_recv.at[slot], to) for slot, to in plan]
    for copy in t:
        copy.start()

    def taps(gap):
        weights = jnp.zeros(gap.shape, F32)
        for n in range(5):
            weights = jnp.where(gap == n - 2, BLUR_TAPS[n], weights)
        return weights

    def band(shape, offset):
        i = lax.broadcasted_iota(jnp.int32, shape, 0)
        j = lax.broadcasted_iota(jnp.int32, shape, 1)
        return taps(j - i + offset)

    def dot(a, b):
        a = halves(a)
        both = jnp.dot(jnp.concatenate(a, axis=0), b[0], preferred_element_type=F32)
        return both[:height] + both[height:] + jnp.dot(a[0], b[1], preferred_element_type=F32)

    def fall(above, here, below):
        x = jnp.concatenate([above, here, below], axis=0)
        return sum(BLUR_TAPS[n] * x[height - 2 + n:2 * height - 2 + n] for n in range(5))

    bands = [halves(band((width, width), offset)) for offset in (0, width, -width)]
    for copy in z + y + c + h:
        copy.wait_send()
    for copy in t:
        copy.wait_recv()
    middle = fall(tiles[0], found, tiles[1])
    left = fall(tiles[3], tiles[2], tiles[4]) * lead
    right = fall(tiles[6], tiles[5], tiles[7]) * trail
    out[...] = dot(middle, bands[0]) + dot(left, bands[1]) + dot(right, bands[2])
    for copy in t:
        copy.wait_send()


def shards(feature_two, inner_three, skip_three, out_weight, out_bias, bank_rows, coreset_index):
    height, width, c2 = feature_two.shape
    deep, wide, c3 = skip_three.shape
    n_bank = lax.axis_size("bank")
    cores = coreset_index.shape[0]
    vm = pl.BlockSpec(memory_space=VMEM)
    hbm = pl.BlockSpec(memory_space=pl.ANY)
    dma = pltpu.SemaphoreType.DMA
    return pl.pallas_call(
        roll_map,
        out_shape=jax.ShapeDtypeStruct((height, width), F32),
        in_specs=[hbm] * 4 + [vm, hbm, vm],
        out_specs=vm,
        scratch_shapes=[
            VMEM(feature_two.shape, BF16), VMEM(inner_three.shape, BF16), VMEM(skip_three.shape, BF16),
            VMEM(out_weight.shape, BF16), VMEM(bank_rows.shape, BF16), dma((5,)),
            VMEM((deep, wide, c3), BF16),
            VMEM((16, c2 + c3), BF16),
            VMEM((n_bank, cores, c2 + c3), BF16),
            VMEM((2, width, c2), BF16),
            VMEM((4, wide, c3), BF16),
            VMEM((6, 16, c2 + c3), BF16),
            VMEM((deep + 2, wide, c3), BF16),
            VMEM((height, width, c2 + c3), BF16),
            VMEM((height, 8, width), F32),
            VMEM((height, 8, width), F32),
            VMEM((height, width), F32),
            VMEM((8, height, width), F32),
        ] + [dma((n_bank - 1,))] * 4 + [dma((2 * (n_bank - 1),))] * 2 + [dma((12,))] * 2 + [dma((8,))] * 2,
        compiler_params=pltpu.CompilerParams(
            collective_id=0, has_side_effects=True, vmem_limit_bytes=60 * 2**20),
    )(feature_two, inner_three, skip_three, out_weight, out_bias[None, :], bank_rows, coreset_index[None, :])


def solution(mesh):
    in_specs = (
        P("circ", ("len", "bank"), None),
        P("circ", ("len", "bank"), None),
        P("circ", ("len", "bank"), None),
        P(),
        P(),
        P("bank", None),
        P("bank"),
    )
    out_specs = P("circ", ("len", "bank"))
    return jax.shard_map(shards, mesh=mesh, in_specs=in_specs, out_specs=out_specs, check_vma=False)
```

```python
import math

import jax
import jax.numpy as jnp
from jax import lax
from jax.experimental import pallas as pl
from jax.experimental.pallas import tpu as pltpu
from jax.sharding import PartitionSpec as P

RAW_TAPS = [math.exp(-0.5 * (t - 2) * (t - 2)) for t in range(5)]
BLUR_TAPS = [value / sum(RAW_TAPS) for value in RAW_TAPS]
MESH = pl.DeviceIdType.MESH
F32 = jnp.float32
BF16 = jnp.bfloat16
VMEM = pltpu.VMEM


def places():
    circ, span, bank = (lax.axis_index(a) for a in ("circ", "len", "bank"))
    n_circ, n_len, n_bank = (lax.axis_size(a) for a in ("circ", "len", "bank"))
    up, down = lax.rem(circ + n_circ - 1, n_circ), lax.rem(circ + 1, n_circ)
    total = n_len * n_bank
    flat = span * n_bank + bank
    before, after = lax.rem(flat + total - 1, total), lax.rem(flat + 1, total)
    left = (before // n_bank, lax.rem(before, n_bank))
    right = (after // n_bank, lax.rem(after, n_bank))
    sides = [(circ,) + left, (circ,) + right]
    corners = [(c,) + s for s in (left, right) for c in (up, down)]
    return (up, span, bank), (down, span, bank), sides, corners, flat == 0, flat == total - 1


def meet(devices):
    barrier = pltpu.get_barrier_semaphore()
    for device in devices:
        pl.semaphore_signal(barrier, inc=1, device_id=device, device_id_type=MESH)
    pl.semaphore_wait(barrier, len(devices))


def shift_rows(x, by, edge):
    n = x.shape[0]
    moved = pltpu.roll(x, by % n, 0)
    at = 0 if by == 1 else n - 1
    return jnp.where(lax.broadcasted_iota(jnp.int32, x.shape, 0) == at, edge, moved)


def send(src, dst, s, r, device):
    return pltpu.make_async_remote_copy(src, dst, s, r, device_id=device, device_id_type=MESH)


def halves(x):
    high = x.astype(BF16)
    return [high, (x - high.astype(F32)).astype(BF16)]


def roll_map(feature_in, inner_in, skip_in, weight_in, bias, bank_in, index, out,
             feature, inner, skip, weight, bank_rows, load, layer, pack, cores, f_halo, l_halo, packs, pooled, patches, sizes, bests, scores, tiles,
             z_send, z_recv, y_send, y_recv, c_send, c_recv, h_send, h_recv, t_send, t_recv):
    circ, span, bank = (lax.axis_index(a) for a in ("circ", "len", "bank"))
    n_len, n_bank = lax.axis_size("len"), lax.axis_size("bank")
    up, down, sides, corners, at_start, at_end = places()
    across = lax.rem(span + 2, n_len)
    mate = (span // 2) * 2 + 1 - lax.rem(span, 2)
    z_peers = [(circ, span, lax.rem(bank + d, n_bank)) for d in range(1, n_bank)]
    y_peer, c_peer = (circ, across, bank), (circ, mate, bank)
    pairs = [(bank_in, bank_rows), (inner_in, inner), (weight_in, weight), (skip_in, skip), (feature_in, feature)]
    loads = [pltpu.make_async_copy(src, dst, load.at[n]) for n, (src, dst) in enumerate(pairs)]
    for copy in loads:
        copy.start()
    meet([up, down] + sides + corners + z_peers + [y_peer, c_peer])
    height, width, c2 = feature.shape
    deep, wide, c3 = skip.shape
    piece = cores.shape[1] // n_len

    def rows(owner):
        return pl.ds(pl.multiple_of(owner * piece, piece), piece)

    halo = [
        (layer.at[deep - 1], l_halo.at[1], down), (layer.at[0], l_halo.at[2], up),
        (feature_in.at[height - 1], f_halo.at[0], down), (feature_in.at[0], f_halo.at[1], up),
        (layer.at[deep - 2], l_halo.at[0], down), (layer.at[1], l_halo.at[3], up),
        (pack, packs.at[3], sides[0]), (pack, packs.at[0], sides[1]),
        (pack, packs.at[5], corners[0]), (pack, packs.at[4], corners[1]),
        (pack, packs.at[2], corners[2]), (pack, packs.at[1], corners[3]),
    ]
    h = [send(s, d, h_send.at[i], h_recv.at[i], to) for i, (s, d, to) in enumerate(halo)]

    h[2].start()
    h[3].start()
    chosen = index[...] == lax.broadcasted_iota(jnp.int32, (bank_rows.shape[0], cores.shape[1]), 0)
    loads[0].wait()
    cores[0] = lax.dot_general(jnp.where(chosen, 1.0, 0.0).astype(BF16), bank_rows[...],
                               (((0,), (0,)), ((), ())), preferred_element_type=F32).astype(BF16)
    z = [send(cores.at[0, rows(span)], cores.at[d + 1, rows(span)], z_send.at[d], z_recv.at[d], z_peers[d])
         for d in range(n_bank - 1)]
    for copy in z:
        copy.start()
    for copy in loads[1:]:
        copy.wait()

    sixteen = lax.broadcasted_iota(jnp.int32, (16, c3), 0)
    packed = jnp.zeros((16, c3), F32)
    for r in [deep - 1, 0] + list(range(1, deep - 1)):
        linear = jnp.dot(inner[r], weight[...], preferred_element_type=F32)
        value = jnp.maximum(linear + bias[...] + skip[r].astype(F32), 0.0).astype(BF16)
        layer[r] = value
        value = value.astype(F32)
        for column in (0, 1):
            packed = jnp.where(sixteen == 2 * r + column, value[column:column + 1], packed)
            at = wide - 2 + column
            packed = jnp.where(sixteen == 8 + 2 * r + column, value[at:at + 1], packed)
        if r == deep - 1:
            h[0].start()
        if r == 0:
            h[1].start()
    pack[:, c2:] = packed.astype(BF16)
    sixteen = lax.broadcasted_iota(jnp.int32, (16, c2), 0)
    packed = jnp.zeros((16, c2), F32)
    for r in range(height):
        packed = jnp.where(sixteen == r, feature[r, 0:16].astype(F32)[0:1], packed)
        packed = jnp.where(sixteen == 8 + r, feature[r, width - 16:width].astype(F32)[15:16], packed)
    pack[:, :c2] = packed.astype(BF16)
    for copy in h[6:]:
        copy.start()

    lead = jnp.where(at_start, 0.0, 1.0)
    trail = jnp.where(at_end, 0.0, 1.0)
    for copy in h[6:]:
        copy.wait_recv()
    pk = [packs[i].astype(F32) * (lead if i < 3 else trail) for i in range(6)]

    def f_row(r):
        return (f_halo[0] if r < 0 else f_halo[1] if r >= height else feature[r]).astype(F32)

    def l_row(r):
        return (l_halo[r + 2] if r < 0 else l_halo[2 + r - deep] if r >= deep else layer[r]).astype(F32)

    def pick(side, r, depth):
        which = side * 3 + (1 if r < 0 else 2 if r >= depth else 0)
        return pk[which], r % depth

    def f_edge(side, r):
        package, row = pick(side, r, height)
        at = row + (8 if side == 0 else 0)
        return package[at:at + 1, :c2]

    def l_edge(side, r, column):
        package, row = pick(side, r, deep)
        at = 2 * row + column + (8 if side == 0 else 0)
        return package[at:at + 1, c2:]

    q_lead, q_trail = {}, {}

    def pool_three(k):
        s = l_row(k - 1) + l_row(k) + l_row(k + 1)
        e = [[sum(l_edge(side, k + t, column) for t in (-1, 0, 1)) for column in (0, 1)] for side in (0, 1)]
        q = ((s + shift_rows(s, 1, e[0][1]) + shift_rows(s, -1, e[1][0])) * (1.0 / 9.0)).astype(BF16)
        pooled[k + 1] = q
        first = ((e[0][0] + e[0][1] + s[0:1]) * (1.0 / 9.0)).astype(BF16).astype(F32)
        last = ((s[wide - 1:wide] + e[1][0] + e[1][1]) * (1.0 / 9.0)).astype(BF16).astype(F32)
        qf = q.astype(F32)
        q_lead[k + 1] = jnp.where(at_start, qf[0:1], first)
        q_trail[k + 1] = jnp.where(at_end, qf[wide - 1:wide], last)

    i = lax.broadcasted_iota(jnp.int32, (width, wide), 0)
    j = lax.broadcasted_iota(jnp.int32, (width, wide), 1)
    k = i // 2
    near = k - 1 + 2 * (i % 2)
    stretch = jnp.where(j == k, 0.75, jnp.where(j == near, 0.25, 0.0)).astype(F32)
    main_w = (0.75 * stretch).astype(BF16)
    side_w = (0.25 * stretch).astype(BF16)
    row_id = lax.broadcasted_iota(jnp.int32, (8, c3), 0)
    ones = jnp.ones((8, 256), BF16)

    def make_patch(r):
        s = f_row(r - 1) + f_row(r) + f_row(r + 1)
        e = [sum(f_edge(side, r + t) for t in (-1, 0, 1)) for side in (0, 1)]
        two = ((s + shift_rows(s, 1, e[0]) + shift_rows(s, -1, e[1])) * (1.0 / 9.0)).astype(BF16)
        a = r // 2 + 1
        b = a + (1 if r % 2 else -1)
        u = jnp.dot(main_w, pooled[a], preferred_element_type=F32)
        u = u + jnp.dot(side_w, pooled[b], preferred_element_type=F32)
        begin = 0.25 * (0.75 * q_lead[a] + 0.25 * q_lead[b])
        end = 0.25 * (0.75 * q_trail[a] + 0.25 * q_trail[b])
        u = jnp.concatenate([u[:8] + jnp.where(row_id == 0, begin, 0.0), u[8:width - 8],
                             u[width - 8:] + jnp.where(row_id == 7, end, 0.0)], axis=0)
        patch = jnp.concatenate([two, u.astype(BF16)], axis=1)
        patches[r] = patch
        wide_patch = patch.astype(F32)
        square = wide_patch * wide_patch
        folded = sum(square[:, t:t + 128] for t in range(0, c2 + c3, 128))
        sizes[r] = lax.dot_general(ones, jnp.concatenate(halves(folded), axis=1), (((1,), (1,)), ((), ())),
                                   preferred_element_type=F32)

    for k in range(1, deep - 1):
        pool_three(k)
    for r in range(3, height - 3):
        make_patch(r)
    y, c = [], []
    for d in range(n_bank - 1):
        z[d].wait_recv()
        here = cores.at[d + 1, rows(span)]
        y.append(send(here, here, y_send.at[d], y_recv.at[d], y_peer))
        y[-1].start()
        c.append(send(here, here, c_send.at[d], c_recv.at[d], c_peer))
        c[-1].start()
    h[4].start()
    h[5].start()
    h[0].wait_recv()
    h[1].wait_recv()
    pool_three(0)
    pool_three(deep - 1)
    for r in [1, 2, height - 3, height - 2]:
        make_patch(r)
    for d in range(n_bank - 1):
        y[d].wait_recv()
        here = cores.at[d + 1, rows(across)]
        e = n_bank - 1 + d
        c.append(send(here, here, c_send.at[e], c_recv.at[e], c_peer))
        c[-1].start()
    norms = []

    def score_row(r, parts):
        patch = patches[r]
        best = None
        for part in parts:
            product = lax.dot_general(cores[part], patch, (((1,), (1,)), ((), ())), preferred_element_type=F32)
            low = jnp.min(norms[part] - 2.0 * product, axis=0, keepdims=True)
            best = low if best is None else jnp.minimum(best, low)
        best = jnp.broadcast_to(best, bests.shape[1:])
        bests[r] = best if parts[0] == 0 else jnp.minimum(bests[r], best)

    def score_rows(first, last, step, parts):
        def body(n, carry):
            score_row(first + step * n, parts)
            return carry

        lax.fori_loop(0, last, body, 0)

    for part in range(n_bank):
        if part:
            c[part - 1].wait_recv()
            c[n_bank - 2 + part].wait_recv()
        wide_core = cores[part].astype(F32)
        norms.append(jnp.sum(wide_core * wide_core, axis=1, keepdims=True))
        score_rows(1, height - 2, 1, [part])
    for copy in h[2:6]:
        copy.wait_recv()
    pool_three(-1)
    pool_three(deep)
    make_patch(0)
    make_patch(height - 1)
    score_rows(0, 2, height - 1, list(range(n_bank)))

    eight = lax.broadcasted_iota(jnp.int32, (height, width), 0)
    found = jnp.zeros((height, width), F32)
    for r in range(height):
        found = jnp.where(eight == r, (sizes[r][0:1] + bests[r][0:1]) / (c2 + c3), found)
    scores[...] = found
    plan = [(0, down), (1, up), (5, sides[0]), (2, sides[1]), (7, corners[0]), (6, corners[1]),
            (4, corners[2]), (3, corners[3])]
    t = [send(scores, tiles.at[slot], t_send.at[slot], t_recv.at[slot], to) for slot, to in plan]
    for copy in t:
        copy.start()

    def taps(gap):
        weights = jnp.zeros(gap.shape, F32)
        for n in range(5):
            weights = jnp.where(gap == n - 2, BLUR_TAPS[n], weights)
        return weights

    def band(shape, offset):
        i = lax.broadcasted_iota(jnp.int32, shape, 0)
        j = lax.broadcasted_iota(jnp.int32, shape, 1)
        return taps(j - i + offset)

    def dot(a, b):
        a = halves(a)
        both = jnp.dot(jnp.concatenate(a, axis=0), b[0], preferred_element_type=F32)
        return both[:height] + both[height:] + jnp.dot(a[0], b[1], preferred_element_type=F32)

    def fall(above, here, below):
        x = jnp.concatenate([above, here, below], axis=0)
        return sum(BLUR_TAPS[n] * x[height - 2 + n:2 * height - 2 + n] for n in range(5))

    bands = [halves(band((width, width), offset)) for offset in (0, width, -width)]
    for copy in z + y + c + h:
        copy.wait_send()
    for copy in t:
        copy.wait_recv()
    middle = fall(tiles[0], found, tiles[1])
    left = fall(tiles[3], tiles[2], tiles[4]) * lead
    right = fall(tiles[6], tiles[5], tiles[7]) * trail
    out[...] = dot(middle, bands[0]) + dot(left, bands[1]) + dot(right, bands[2])
    for copy in t:
        copy.wait_send()


def shards(feature_two, inner_three, skip_three, out_weight, out_bias, bank_rows, coreset_index):
    height, width, c2 = feature_two.shape
    deep, wide, c3 = skip_three.shape
    n_bank = lax.axis_size("bank")
    cores = coreset_index.shape[0]
    vm = pl.BlockSpec(memory_space=VMEM)
    hbm = pl.BlockSpec(memory_space=pl.ANY)
    dma = pltpu.SemaphoreType.DMA
    return pl.pallas_call(
        roll_map,
        out_shape=jax.ShapeDtypeStruct((height, width), F32),
        in_specs=[hbm] * 4 + [vm, hbm, vm],
        out_specs=vm,
        scratch_shapes=[
            VMEM(feature_two.shape, BF16), VMEM(inner_three.shape, BF16), VMEM(skip_three.shape, BF16),
            VMEM(out_weight.shape, BF16), VMEM(bank_rows.shape, BF16), dma((5,)),
            VMEM((deep, wide, c3), BF16),
            VMEM((16, c2 + c3), BF16),
            VMEM((n_bank, cores, c2 + c3), BF16),
            VMEM((2, width, c2), BF16),
            VMEM((4, wide, c3), BF16),
            VMEM((6, 16, c2 + c3), BF16),
            VMEM((deep + 2, wide, c3), BF16),
            VMEM((height, width, c2 + c3), BF16),
            VMEM((height, 8, width), F32),
            VMEM((height, 8, width), F32),
            VMEM((height, width), F32),
            VMEM((8, height, width), F32),
        ] + [dma((n_bank - 1,))] * 4 + [dma((2 * (n_bank - 1),))] * 2 + [dma((12,))] * 2 + [dma((8,))] * 2,
        compiler_params=pltpu.CompilerParams(
            collective_id=0, has_side_effects=True, vmem_limit_bytes=60 * 2**20),
    )(feature_two, inner_three, skip_three, out_weight, out_bias[None, :], bank_rows, coreset_index[None, :])


def solution(mesh):
    in_specs = (
        P("circ", ("len", "bank"), None),
        P("circ", ("len", "bank"), None),
        P("circ", ("len", "bank"), None),
        P(),
        P(),
        P("bank", None),
        P("bank"),
    )
    out_specs = P("circ", ("len", "bank"))
    return jax.shard_map(shards, mesh=mesh, in_specs=in_specs, out_specs=out_specs, check_vma=False)
```
